32 devices in a mesh: sta: 16 (over z, y, core), band: 2 (over x).
Axes of the slice: x: 2, y: 2, z: 4, core: 2. Of those that a mesh axis runs over, the one named last changes fastest.
Arguments:
- spectra: bfloat16 [256, 2, 2, 4096], P('sta', None, None, 'band')
- flags: int32 [256, 2], P('sta'), may hold values 0 or 1
- passband: int32 [256, 2], P('sta'), may hold values from 0 to 4096, as said below
Outputs:
- correlation: float32 [256, 32, 256], P('sta', None, 'band')
The draws below stay inside these ranges and needn't reach their ends.
Inputs may be any that keep to these rules, and one draw needn't show every extreme that they name: 0 <= passband[s, 0] < 512 and 3584 < passband[s, 1]; some station starts at 0 and some ends at 4096.
All inputs are finite; a program needn't handle non-finite values. No bound on the sum of `flags` on one device may be relied on, other than what follows from the above.
Results may differ from the reference program's by a relative error of at most 0.0044.
Values may be sent and summed in bfloat16 or wider, within the bound.
A program may use at most 64 MiB of HBM per device.

```python
import math
import jax
import jax.numpy as jnp
from jax import lax

SPD = 16
SEG = 2
FREQ = 4096
LAGS = 32
STATIONS = 256
N_STA = 16


def draw_spectra(key, part):
    key_station = jax.random.fold_in(key, 0)
    key_rough = jax.random.fold_in(key, 1)
    key_base = jax.random.fold_in(key, 2)
    key_silent = jax.random.fold_in(key, 4)
    key_pick = jax.random.fold_in(key, 5)
    full_shape = (STATIONS, SEG, 2, FREQ)
    station_scale = jnp.exp(jnp.log(10.0) * jax.random.uniform(key_station, (STATIONS, 1, 1, 1)))
    colored = jnp.exp(jnp.log(10.0) * jnp.arange(FREQ, dtype=jnp.float32) / FREQ)
    roughness = jnp.exp(jnp.log(2.0) * jax.random.uniform(key_rough, full_shape, minval=-1.0, maxval=1.0))
    noise_base = jax.random.normal(key_base, full_shape)
    silent = jax.random.bernoulli(key_silent, 0.125, (STATIONS, SEG))
    chosen = jax.random.randint(key_pick, (), 0, STATIONS * SEG)
    segment_ids = jnp.arange(STATIONS * SEG, dtype=jnp.int32).reshape(STATIONS, SEG)
    silent = silent | (segment_ids == chosen)
    alive = jnp.where(silent, 0.0, 1.0).astype(jnp.float32)[:, :, None, None]
    return (noise_base * roughness * station_scale * colored * alive).astype(jnp.bfloat16)


def draw_passband(key, part):
    key_lower, key_upper = jax.random.split(key, 2)
    lower_edge = jax.random.randint(key_lower, (STATIONS,), 0, FREQ // 8)
    lower_edge = lower_edge - jnp.min(lower_edge)
    upper_cut = jax.random.randint(key_upper, (STATIONS,), 0, FREQ // 8)
    upper_cut = upper_cut - jnp.min(upper_cut)
    return jnp.stack([lower_edge, FREQ - upper_cut], axis=1).astype(jnp.int32)


def place_ends(values, own_key, least, high):
    longest = values.shape.index(max(values.shape))
    spots = []
    for shift in (0, 1):
        where = [jax.random.randint(jax.random.fold_in(own_key, axis), (), 0, length) for axis, length in enumerate(values.shape)]
        where[longest] = (where[longest] + shift) % values.shape[longest]
        spots.append(tuple(where))
    return values.at[spots[0]].set(least).at[spots[1]].set(high)


def setup_inputs(seed: int = 0) -> dict:
    key_of = jax.random.split(jax.random.key(seed), 4)
    spectra = draw_spectra(jax.random.fold_in(key_of[3], 71), 0)
    flags = place_ends((jax.random.randint(key_of[1], (STATIONS, SEG), 0, 4) < 3).astype(jnp.int32), jax.random.fold_in(key_of[1], 1), 0, 1)
    passband = draw_passband(jax.random.fold_in(key_of[3], 71), 0)
    return dict(spectra=spectra, flags=flags, passband=passband)


def passband_mask(passband, freq_index):
    lower_ok = freq_index[None, :] >= passband[:, 0:1]
    upper_ok = freq_index[None, :] < passband[:, 1:2]
    return (lower_ok & upper_ok).astype(jnp.float32)

def lag_tables(freq_index):
    lag_index = jnp.arange(LAGS, dtype=jnp.int32) - LAGS // 2
    turns = jnp.mod(lag_index[:, None] * freq_index[None, :], FREQ)
    phases = turns.astype(jnp.float32) * (2.0 * math.pi / FREQ)
    return (jnp.cos(phases), jnp.sin(phases))

def rotate(whitened, cosine, sine_table):
    real_part = whitened[:, :, 0, :].astype(jnp.float32)[:, None]
    imag_part = whitened[:, :, 1, :].astype(jnp.float32)[:, None]
    cos_b = cosine[None, :, None, :]
    sin_b = sine_table[None, :, None, :]
    rot_real = real_part * cos_b - imag_part * sin_b
    rot_imag = imag_part * cos_b + real_part * sin_b
    return jnp.stack([rot_real, rot_imag], axis=3).astype(jnp.bfloat16)

def reference(spectra, flags, passband):
    freq_index = jnp.arange(FREQ, dtype=jnp.int32)
    kept = passband_mask(passband, freq_index)
    values = spectra.astype(jnp.float32)
    energy = lax.optimization_barrier(jnp.sum(values * values * kept[:, None, None, :], axis=(2, 3)))
    band_width = (passband[:, 1] - passband[:, 0]).astype(jnp.float32)
    root_mean = jnp.sqrt(energy / band_width[:, None] + 1e-06)
    valid = flags.astype(jnp.float32)
    whitened = (values * (kept[:, None, None, :] * valid[:, :, None, None] / root_mean[:, :, None, None])).astype(jnp.bfloat16)
    cosine, sine_table = lag_tables(freq_index)
    flat_rows = whitened.reshape(STATIONS, SEG * 2 * FREQ)
    groups = whitened.reshape(N_STA, SPD, SEG, 2, FREQ)

    def one_block(group):
        rotated = rotate(group, cosine, sine_table).reshape(SPD * LAGS, SEG * 2 * FREQ)
        return jnp.dot(rotated, flat_rows.T, preferred_element_type=jnp.float32)
    stacks = lax.map(one_block, groups).reshape(STATIONS, LAGS, STATIONS)
    pairs = jnp.dot(valid, valid.T, preferred_element_type=jnp.float32)
    return stacks / (jnp.maximum(pairs, 1.0)[:, None, :] * math.sqrt(FREQ))
```

```python
import functools
import math

import jax
import jax.numpy as jnp
from jax import lax
from jax.experimental import pallas as pl
from jax.experimental.pallas import tpu as pltpu
from jax.sharding import PartitionSpec as P

FREQ = 4096
LAGS = 32
SEG = 2
PIECES = 4
EXT = 128
MESH = pl.DeviceIdType.MESH


def station_of(position, core, chips):
    half = chips // 2
    if chips == 8:
        chip = jnp.where(position < half, 2 * position, 2 * (chips - 1 - position) + 1)
    else:
        chip = jnp.where(position < half, position, half + (chips - 1 - position))
    return 2 * chip + core


def position_of(chip, chips):
    half = chips // 2
    if chips == 8:
        return jnp.where(chip % 2 == 0, chip // 2, chips - 1 - chip // 2)
    return jnp.where(chip < half, chip, chips - 1 - (chip - half))


def kernel(
    n, nb, x_ref, flags_ref, band_ref, out_ref,
    w, rot, cos_ref, sin_ref, acc, energies, part, got,
    ring_send, ring_recv, sib_send, sib_recv, en_send, en_recv, part_send, part_recv,
):
    rows, wide = x_ref.shape
    freq = wide // (2 * SEG)
    half = freq // 2
    depth = 2 * half
    chips = n // 2
    share = n * rows // nb
    me = lax.axis_index("sta")
    band = lax.axis_index("band")
    core = lax.rem(me, 2)
    pos = position_of(me // 2, chips)
    sibling = me + 1 - 2 * core

    def at_pos(offset, own_core):
        return station_of(lax.rem(pos + offset + chips, chips), own_core, chips)

    right, left = at_pos(1, core), at_pos(-1, core)

    barrier = pltpu.get_barrier_semaphore()
    for other in (right, left, sibling):
        pl.semaphore_signal(barrier, inc=1, device_id={"sta": other}, device_id_type=MESH)
    for k in range(1, nb):
        pl.semaphore_signal(
            barrier, inc=1, device_id={"band": lax.rem(band + k, nb)}, device_id_type=MESH
        )

    f_index = band * freq + lax.broadcasted_iota(jnp.int32, (rows, freq), 1)
    kept = (f_index >= band_ref[:, 0:1]) & (f_index < band_ref[:, 1:2])
    lane = lax.broadcasted_iota(jnp.int32, (rows, EXT), 1)
    sums, undo = [], []
    for g in range(SEG):
        vals = []
        for c in range(2):
            start = (g * 2 + c) * freq
            v = x_ref[:, start:start + freq].astype(jnp.float32)
            vals.append(jnp.where(kept, v, 0.0))
        e = jnp.sum(vals[0] * vals[0] + vals[1] * vals[1], axis=1, keepdims=True)
        big = jnp.where(e < 3.0e38, 2.0 ** -40, 0.0)
        fac = jnp.where(e < 2.0 ** -60, 2.0 ** 40, jnp.where(e > 2.0 ** 80, big, 1.0))
        undo.append(jnp.where(e < 2.0 ** -60, 2.0 ** -40, jnp.where(e > 2.0 ** 80, 2.0 ** 40, 1.0)))
        sums.append(e)
        for h in range(2):
            for c in range(2):
                w[2 * g + h, me, :, c * half:(c + 1) * half] = (
                    vals[c][:, h * half:(h + 1) * half] * fac
                ).astype(jnp.bfloat16)
    energies[band] = jnp.where(lane == 0, sums[0], jnp.where(lane == 1, sums[1], 0.0))

    pl.semaphore_wait(barrier, 3 + nb - 1)

    en_copies = []
    for k in range(1, nb):
        en_copies.append(pltpu.make_async_remote_copy(
            src_ref=energies.at[band], dst_ref=energies.at[band],
            send_sem=en_send.at[k], recv_sem=en_recv.at[k],
            device_id={"band": lax.rem(band + k, nb)}, device_id_type=MESH,
        ))
        en_copies[-1].start()

    def view(p, s):
        return w.at[p, s] if p == PIECES - 1 else w.at[p, s, :, 0:depth]

    def ring(p, way, t, s):
        return pltpu.make_async_remote_copy(
            src_ref=view(p, s), dst_ref=view(p, s),
            send_sem=ring_send.at[way, p, t], recv_sem=ring_recv.at[way, p, t],
            device_id={"sta": right if way == 0 else left}, device_id_type=MESH,
        )

    def across(p, k, s):
        return pltpu.make_async_remote_copy(
            src_ref=view(p, s), dst_ref=view(p, s),
            send_sem=sib_send.at[p, k], recv_sem=sib_recv.at[p, k],
            device_id={"sta": sibling}, device_id_type=MESH,
        )

    long = chips // 2
    hops = [(long, chips - 1 - long) if p % 2 == 0 else (chips - 1 - long, long)
            for p in range(PIECES)]
    sent = []

    def go(copy):
        copy.start()
        sent.append(copy)

    def send_own(p):
        for way in range(2):
            if hops[p][way] > 0:
                go(ring(p, way, 0, me))
        go(across(p, 0, me))

    for p in range(PIECES - 1):
        send_own(p)

    for k in range(1, nb):
        source = lax.rem(band + nb - k, nb)
        pltpu.make_async_remote_copy(
            src_ref=energies.at[source], dst_ref=energies.at[source],
            send_sem=en_send.at[k], recv_sem=en_recv.at[k],
            device_id={"band": source}, device_id_type=MESH,
        ).wait_recv()
    total = energies[0]
    for k in range(1, nb):
        total = total + energies[k]
    width = (band_ref[:, 1:2] - band_ref[:, 0:1]).astype(jnp.float32)
    ext = jnp.zeros((rows, EXT), jnp.float32)
    own = []
    for g in range(SEG):
        valid = flags_ref[:, g:g + 1].astype(jnp.float32)
        factor = valid / jnp.sqrt(total[:, g:g + 1] / width + 1e-06) * undo[g]
        own.append(factor)
        rest = factor
        for i in range(3):
            term = rest.astype(jnp.bfloat16).astype(jnp.float32)
            rest = rest - term
            ext = jnp.where(lane == 3 * g + i, term, ext)
        ext = jnp.where(lane == 6 + g, valid, ext)
    w[PIECES - 1, me, :, depth:depth + EXT] = ext.astype(jnp.bfloat16)
    send_own(PIECES - 1)

    @pl.loop(0, freq // 128)
    def _(j):
        cols = pl.ds(pl.multiple_of(j * 128, 128), 128)
        lag = lax.broadcasted_iota(jnp.int32, (LAGS, 128), 0) - LAGS // 2
        f = band * freq + j * 128 + lax.broadcasted_iota(jnp.int32, (LAGS, 128), 1)
        turns = ((lag * f + FREQ // 2) & (FREQ - 1)) - FREQ // 2
        phase = turns.astype(jnp.float32) * (2.0 * math.pi / FREQ)
        cos_ref[:, cols] = jnp.cos(phase)
        sin_ref[:, cols] = jnp.sin(phase)

    def rotate(p):
        h = p % 2

        @pl.loop(0, half // 128)
        def _(j):
            at = pl.multiple_of(j * 128, 128)
            table = pl.ds(pl.multiple_of(h * half + j * 128, 128), 128)
            cosine, sine = cos_ref[:, table], sin_ref[:, table]
            re = w[p, me, :, pl.ds(at, 128)].astype(jnp.float32)
            im = w[p, me, :, pl.ds(pl.multiple_of(half + j * 128, 128), 128)].astype(jnp.float32)
            for a in range(rows):
                r, i = re[a:a + 1], im[a:a + 1]
                lines = slice(a * LAGS, (a + 1) * LAGS)
                rot[p, lines, pl.ds(at, 128)] = (r * cosine - i * sine).astype(jnp.bfloat16)
                rot[p, lines, pl.ds(pl.multiple_of(half + j * 128, 128), 128)] = (
                    i * cosine + r * sine
                ).astype(jnp.bfloat16)

    def hop(p, t):
        for way in range(2):
            if t <= hops[p][way]:
                s = at_pos(-t if way == 0 else t, core)
                ring(p, way, t - 1, s).wait_recv()
                if t < hops[p][way]:
                    go(ring(p, way, t, s))
                go(across(p, t if way == 0 else hops[p][0] + t, s))

    def multiply(p):
        g = p // 2
        for k in range(chips):
            t = k if k <= hops[p][0] else k - hops[p][0]
            s = at_pos(-t if k <= hops[p][0] else t, 1 - core)
            across(p, k, s).wait_recv()
        step = min(depth, 512)

        @pl.loop(0, depth // step)
        def _(j):
            cols = pl.ds(pl.multiple_of(j * step, step), step)
            term = lax.dot_general(
                rot[p, :, cols], w[p, :, :, cols].reshape(n * rows, step),
                (((1,), (1,)), ((), ())), preferred_element_type=jnp.float32,
            )
            if p % 2 == 0:
                @pl.when(j == 0)
                def _():
                    acc[g] = term

                @pl.when(j > 0)
                def _():
                    acc[g] += term
            else:
                acc[g] += term

    for t in range(1, long + 1):
        for p in range(PIECES):
            hop(p, t)
            if t == 1:
                rotate(p)
            if t == long:
                multiply(p)

    ext_all = w[PIECES - 1, :, :, depth:depth + EXT].reshape(n * rows, EXT)
    row = lax.broadcasted_iota(jnp.int32, (16, EXT), 0)
    col = lax.broadcasted_iota(jnp.int32, (16, EXT), 1)
    pick = ((row < SEG) & (col >= 3 * row) & (col < 3 * row + 3)).astype(jnp.float32)
    nt = (((1,), (1,)), ((), ()))
    theirs = lax.dot_general(
        pick.astype(jnp.bfloat16), ext_all, nt, preferred_element_type=jnp.float32
    )
    flag_cols = jnp.where((lane >= 6) & (lane < 6 + SEG), ext, 0.0).astype(jnp.bfloat16)
    pairs = lax.dot_general(flag_cols, ext_all, nt, preferred_element_type=jnp.float32)
    denominator = 1.0 / (jnp.maximum(pairs, 1.0) * math.sqrt(FREQ))
    weight = [own[g] * theirs[g:g + 1] * denominator for g in range(SEG)]

    for q in range(nb):
        cols = slice(q * share, (q + 1) * share)
        for a in range(rows):
            lines = slice(a * LAGS, (a + 1) * LAGS)
            part[q, lines] = (
                acc[0, lines, cols] * weight[0][a:a + 1, cols]
                + acc[1, lines, cols] * weight[1][a:a + 1, cols]
            )
    copies = []
    for k in range(1, nb):
        target = lax.rem(band + k, nb)
        copies.append(pltpu.make_async_remote_copy(
            src_ref=part.at[target], dst_ref=got.at[k],
            send_sem=part_send.at[k], recv_sem=part_recv.at[k],
            device_id={"band": target}, device_id_type=MESH,
        ))
        copies[-1].start()
    for copy in sent + en_copies:
        copy.wait_send()
    for copy in copies:
        copy.wait()
    result = part[band]
    for k in range(1, nb):
        result = result + got[k]
    out_ref[...] = result


def solution(mesh):
    n, nb = mesh.shape["sta"], mesh.shape["band"]

    def local(spectra, flags, passband):
        rows, _, _, freq = spectra.shape
        share = n * rows // nb
        depth = freq
        vmem = pl.BlockSpec(memory_space=pltpu.VMEM)
        chips = n // 2
        dma = pltpu.SemaphoreType.DMA
        out = pl.pallas_call(
            functools.partial(kernel, n, nb),
            out_shape=jax.ShapeDtypeStruct((rows * LAGS, share), jnp.float32),
            in_specs=[vmem] * 3,
            out_specs=vmem,
            scratch_shapes=[
                pltpu.VMEM((PIECES, n, rows, depth + EXT), jnp.bfloat16),
                pltpu.VMEM((PIECES, rows * LAGS, depth), jnp.bfloat16),
                pltpu.VMEM((LAGS, freq), jnp.float32),
                pltpu.VMEM((LAGS, freq), jnp.float32),
                pltpu.VMEM((SEG, rows * LAGS, n * rows), jnp.float32),
                pltpu.VMEM((nb, rows, EXT), jnp.float32),
                pltpu.VMEM((nb, rows * LAGS, share), jnp.float32),
                pltpu.VMEM((nb, rows * LAGS, share), jnp.float32),
                dma((2, PIECES, chips)), dma((2, PIECES, chips)),
                dma((PIECES, chips)), dma((PIECES, chips)),
                dma((nb,)), dma((nb,)), dma((nb,)), dma((nb,)),
            ],
            compiler_params=pltpu.CompilerParams(
                collective_id=0, has_side_effects=True, vmem_limit_bytes=48 * 1024 * 1024
            ),
        )(spectra.reshape(rows, SEG * 2 * freq), flags, passband)
        return out.reshape(rows, LAGS, share)

    placed = (P("sta", None, None, "band"), P("sta", None), P("sta", None))
    return jax.shard_map(
        local, mesh=mesh, in_specs=placed, out_specs=P("sta", None, "band"), check_vma=False
    )
```

```python
import functools
import math

import jax
import jax.numpy as jnp
from jax import lax
from jax.experimental import pallas as pl
from jax.experimental.pallas import tpu as pltpu
from jax.sharding import PartitionSpec as P

FREQ = 4096
LAGS = 32
SEG = 2
PIECES = 4
EXT = 128
MESH = pl.DeviceIdType.MESH


def station_of(position, core, chips):
    half = chips // 2
    if chips == 8:
        chip = jnp.where(position < half, 2 * position, 2 * (chips - 1 - position) + 1)
    else:
        chip = jnp.where(position < half, position, half + (chips - 1 - position))
    return 2 * chip + core


def position_of(chip, chips):
    half = chips // 2
    if chips == 8:
        return jnp.where(chip % 2 == 0, chip // 2, chips - 1 - chip // 2)
    return jnp.where(chip < half, chip, chips - 1 - (chip - half))


def kernel(
    n, nb, x_ref, flags_ref, band_ref, out_ref,
    w, rot, cos_ref, sin_ref, acc, energies, weight, part, got,
    ring_send, ring_recv, sib_send, sib_recv, en_send, en_recv, part_send, part_recv,
):
    rows, wide = x_ref.shape
    freq = wide // (2 * SEG)
    half = freq // 2
    depth = 2 * half
    chips = n // 2
    share = n * rows // nb
    me = lax.axis_index("sta")
    band = lax.axis_index("band")
    core = lax.rem(me, 2)
    pos = position_of(me // 2, chips)
    sibling = me + 1 - 2 * core

    def at_pos(offset, own_core):
        return station_of(lax.rem(pos + offset + chips, chips), own_core, chips)

    right, left = at_pos(1, core), at_pos(-1, core)

    barrier = pltpu.get_barrier_semaphore()
    for other in (right, left, sibling):
        pl.semaphore_signal(barrier, inc=1, device_id={"sta": other}, device_id_type=MESH)
    for k in range(1, nb):
        pl.semaphore_signal(
            barrier, inc=1, device_id={"band": lax.rem(band + k, nb)}, device_id_type=MESH
        )

    f_index = band * freq + lax.broadcasted_iota(jnp.int32, (rows, freq), 1)
    kept = (f_index >= band_ref[:, 0:1]) & (f_index < band_ref[:, 1:2])
    lane = lax.broadcasted_iota(jnp.int32, (rows, EXT), 1)
    sums, undo = [], []
    for g in range(SEG):
        vals = []
        for c in range(2):
            start = (g * 2 + c) * freq
            v = x_ref[:, start:start + freq].astype(jnp.float32)
            vals.append(jnp.where(kept, v, 0.0))
        e = jnp.sum(vals[0] * vals[0] + vals[1] * vals[1], axis=1, keepdims=True)
        big = jnp.where(e < 3.0e38, 2.0 ** -40, 0.0)
        fac = jnp.where(e < 2.0 ** -60, 2.0 ** 40, jnp.where(e > 2.0 ** 80, big, 1.0))
        undo.append(jnp.where(e < 2.0 ** -60, 2.0 ** -40, jnp.where(e > 2.0 ** 80, 2.0 ** 40, 1.0)))
        sums.append(e)
        for h in range(2):
            for c in range(2):
                w[2 * g + h, me, :, c * half:(c + 1) * half] = (
                    vals[c][:, h * half:(h + 1) * half] * fac
                ).astype(jnp.bfloat16)
    energies[band] = jnp.where(lane == 0, sums[0], jnp.where(lane == 1, sums[1], 0.0))

    pl.semaphore_wait(barrier, 3 + nb - 1)

    en_copies = []
    for k in range(1, nb):
        en_copies.append(pltpu.make_async_remote_copy(
            src_ref=energies.at[band], dst_ref=energies.at[band],
            send_sem=en_send.at[k], recv_sem=en_recv.at[k],
            device_id={"band": lax.rem(band + k, nb)}, device_id_type=MESH,
        ))
        en_copies[-1].start()

    def view(p, s):
        return w.at[p, s] if p == PIECES - 1 else w.at[p, s, :, 0:depth]

    def ring(p, way, t, s):
        return pltpu.make_async_remote_copy(
            src_ref=view(p, s), dst_ref=view(p, s),
            send_sem=ring_send.at[way, p, t], recv_sem=ring_recv.at[way, p, t],
            device_id={"sta": right if way == 0 else left}, device_id_type=MESH,
        )

    def across(p, k, s):
        return pltpu.make_async_remote_copy(
            src_ref=view(p, s), dst_ref=view(p, s),
            send_sem=sib_send.at[p, k], recv_sem=sib_recv.at[p, k],
            device_id={"sta": sibling}, device_id_type=MESH,
        )

    long = chips // 2
    hops = [(long, chips - 1 - long) if p % 2 == 0 else (chips - 1 - long, long)
            for p in range(PIECES)]
    sent = []

    def go(copy):
        copy.start()
        sent.append(copy)

    def send_own(p):
        for way in range(2):
            if hops[p][way] > 0:
                go(ring(p, way, 0, me))
        go(across(p, 0, me))

    send_own(0)
    send_own(1)

    for k in range(1, nb):
        source = lax.rem(band + nb - k, nb)
        pltpu.make_async_remote_copy(
            src_ref=energies.at[source], dst_ref=energies.at[source],
            send_sem=en_send.at[k], recv_sem=en_recv.at[k],
            device_id={"band": source}, device_id_type=MESH,
        ).wait_recv()
    total = energies[0]
    for k in range(1, nb):
        total = total + energies[k]
    width = (band_ref[:, 1:2] - band_ref[:, 0:1]).astype(jnp.float32)
    ext = jnp.zeros((rows, EXT), jnp.float32)
    own = []
    for g in range(SEG):
        valid = flags_ref[:, g:g + 1].astype(jnp.float32)
        factor = valid / jnp.sqrt(total[:, g:g + 1] / width + 1e-06) * undo[g]
        own.append(factor)
        rest = factor
        for i in range(3):
            term = rest.astype(jnp.bfloat16).astype(jnp.float32)
            rest = rest - term
            ext = jnp.where(lane == 3 * g + i, term, ext)
        ext = jnp.where(lane == 6 + g, valid, ext)
    w[PIECES - 1, me, :, depth:depth + EXT] = ext.astype(jnp.bfloat16)

    @pl.loop(0, freq // 128)
    def _(j):
        cols = pl.ds(pl.multiple_of(j * 128, 128), 128)
        lag = lax.broadcasted_iota(jnp.int32, (LAGS, 128), 0) - LAGS // 2
        f = band * freq + j * 128 + lax.broadcasted_iota(jnp.int32, (LAGS, 128), 1)
        turns = ((lag * f + FREQ // 2) & (FREQ - 1)) - FREQ // 2
        phase = turns.astype(jnp.float32) * (2.0 * math.pi / FREQ)
        cos_ref[:, cols] = jnp.cos(phase)
        sin_ref[:, cols] = jnp.sin(phase)

    def rotate(p):
        h = p % 2

        @pl.loop(0, half // 128)
        def _(j):
            at = pl.multiple_of(j * 128, 128)
            table = pl.ds(pl.multiple_of(h * half + j * 128, 128), 128)
            cosine, sine = cos_ref[:, table], sin_ref[:, table]
            re = w[p, me, :, pl.ds(at, 128)].astype(jnp.float32)
            im = w[p, me, :, pl.ds(pl.multiple_of(half + j * 128, 128), 128)].astype(jnp.float32)
            for a in range(rows):
                r, i = re[a:a + 1], im[a:a + 1]
                lines = slice(a * LAGS, (a + 1) * LAGS)
                rot[p, lines, pl.ds(at, 128)] = (r * cosine - i * sine).astype(jnp.bfloat16)
                rot[p, lines, pl.ds(pl.multiple_of(half + j * 128, 128), 128)] = (
                    i * cosine + r * sine
                ).astype(jnp.bfloat16)

    def hop(p, t):
        for way in range(2):
            if t <= hops[p][way]:
                s = at_pos(-t if way == 0 else t, core)
                ring(p, way, t - 1, s).wait_recv()
                if t < hops[p][way]:
                    go(ring(p, way, t, s))
                go(across(p, t if way == 0 else hops[p][0] + t, s))

    def gathered(p):
        for k in range(chips):
            t = k if k <= hops[p][0] else k - hops[p][0]
            s = at_pos(-t if k <= hops[p][0] else t, 1 - core)
            across(p, k, s).wait_recv()

    def multiply(p, lines):
        g = p // 2
        step = min(depth, 512)

        @pl.loop(0, depth // step)
        def _(j):
            cols = pl.ds(pl.multiple_of(j * step, step), step)
            term = lax.dot_general(
                rot[p, lines, cols], w[p, :, :, cols].reshape(n * rows, step),
                (((1,), (1,)), ((), ())), preferred_element_type=jnp.float32,
            )
            if p % 2 == 0:
                @pl.when(j == 0)
                def _():
                    acc[g, lines] = term

                @pl.when(j > 0)
                def _():
                    acc[g, lines] += term
            else:
                acc[g, lines] += term

    order = sorted(
        ((p, t) for p in range(PIECES) for t in range(1, long + 1)),
        key=lambda pt: (pt[0] + pt[1], -pt[0]),
    )
    rotated = 0
    for p, t in order:
        hop(p, t)
        if p == 0 and t + 1 < PIECES:
            send_own(t + 1)
        if p + t > 1 and rotated < PIECES:
            rotate(rotated)
            rotated += 1
        if t == long:
            gathered(p)
            if p < PIECES - 1:
                multiply(p, slice(0, rows * LAGS))

    ext_all = w[PIECES - 1, :, :, depth:depth + EXT].reshape(n * rows, EXT)
    row = lax.broadcasted_iota(jnp.int32, (16, EXT), 0)
    col = lax.broadcasted_iota(jnp.int32, (16, EXT), 1)
    pick = ((row < SEG) & (col >= 3 * row) & (col < 3 * row + 3)).astype(jnp.float32)
    nt = (((1,), (1,)), ((), ()))
    theirs = lax.dot_general(
        pick.astype(jnp.bfloat16), ext_all, nt, preferred_element_type=jnp.float32
    )
    flag_cols = jnp.where((lane >= 6) & (lane < 6 + SEG), ext, 0.0).astype(jnp.bfloat16)
    pairs = lax.dot_general(flag_cols, ext_all, nt, preferred_element_type=jnp.float32)
    denominator = 1.0 / (jnp.maximum(pairs, 1.0) * math.sqrt(FREQ))
    for g in range(SEG):
        weight[g] = own[g] * theirs[g:g + 1] * denominator

    def stack(q, first, last):
        cols = pl.ds(pl.multiple_of(q * share, share), share)
        left_factor, right_factor = weight[0, :, cols], weight[1, :, cols]
        for a in range(first, last):
            lines = slice(a * LAGS, (a + 1) * LAGS)
            part[q, lines] = (
                acc[0, lines, cols] * left_factor[a:a + 1]
                + acc[1, lines, cols] * right_factor[a:a + 1]
            )

    copies = []
    for m in range(2):
        first, last = m * rows // 2, (m + 1) * rows // 2
        lines = slice(first * LAGS, last * LAGS)
        multiply(PIECES - 1, lines)
        for k in range(1, nb):
            target = lax.rem(band + k, nb)
            stack(target, first, last)
            copies.append(pltpu.make_async_remote_copy(
                src_ref=part.at[target, lines], dst_ref=got.at[k, lines],
                send_sem=part_send.at[k, m], recv_sem=part_recv.at[k, m],
                device_id={"band": target}, device_id_type=MESH,
            ))
            copies[-1].start()
    stack(band, 0, rows)
    for copy in sent + en_copies:
        copy.wait_send()
    for m in range(2):
        lines = slice(m * rows // 2 * LAGS, (m + 1) * rows // 2 * LAGS)
        for copy in copies[m * (nb - 1):(m + 1) * (nb - 1)]:
            copy.wait()
        result = part[band, lines]
        for k in range(1, nb):
            result = result + got[k, lines]
        out_ref[lines] = result


def solution(mesh):
    n, nb = mesh.shape["sta"], mesh.shape["band"]

    def local(spectra, flags, passband):
        rows, _, _, freq = spectra.shape
        share = n * rows // nb
        depth = freq
        vmem = pl.BlockSpec(memory_space=pltpu.VMEM)
        chips = n // 2
        dma = pltpu.SemaphoreType.DMA
        out = pl.pallas_call(
            functools.partial(kernel, n, nb),
            out_shape=jax.ShapeDtypeStruct((rows * LAGS, share), jnp.float32),
            in_specs=[vmem] * 3,
            out_specs=vmem,
            scratch_shapes=[
                pltpu.VMEM((PIECES, n, rows, depth + EXT), jnp.bfloat16),
                pltpu.VMEM((PIECES, rows * LAGS, depth), jnp.bfloat16),
                pltpu.VMEM((LAGS, freq), jnp.float32),
                pltpu.VMEM((LAGS, freq), jnp.float32),
                pltpu.VMEM((SEG, rows * LAGS, n * rows), jnp.float32),
                pltpu.VMEM((nb, rows, EXT), jnp.float32),
                pltpu.VMEM((SEG, rows, n * rows), jnp.float32),
                pltpu.VMEM((nb, rows * LAGS, share), jnp.float32),
                pltpu.VMEM((nb, rows * LAGS, share), jnp.float32),
                dma((2, PIECES, chips)), dma((2, PIECES, chips)),
                dma((PIECES, chips)), dma((PIECES, chips)),
                dma((nb,)), dma((nb,)), dma((nb, 2)), dma((nb, 2)),
            ],
            compiler_params=pltpu.CompilerParams(
                collective_id=0, has_side_effects=True, vmem_limit_bytes=48 * 1024 * 1024
            ),
        )(spectra.reshape(rows, SEG * 2 * freq), flags, passband)
        return out.reshape(rows, LAGS, share)

    placed = (P("sta", None, None, "band"), P("sta", None), P("sta", None))
    return jax.shard_map(
        local, mesh=mesh, in_specs=placed, out_specs=P("sta", None, "band"), check_vma=False
    )
```

```python
import functools
import math

import jax
import jax.numpy as jnp
from jax import lax
from jax.experimental import pallas as pl
from jax.experimental.pallas import tpu as pltpu
from jax.sharding import PartitionSpec as P

FREQ = 4096
LAGS = 32
SEG = 2
PIECES = 4
EXT = 128
MESH = pl.DeviceIdType.MESH


def station_of(position, core, chips):
    half = chips // 2
    if chips == 8:
        chip = jnp.where(position < half, 2 * position, 2 * (chips - 1 - position) + 1)
    else:
        chip = jnp.where(position < half, position, half + (chips - 1 - position))
    return 2 * chip + core


def position_of(chip, chips):
    half = chips // 2
    if chips == 8:
        return jnp.where(chip % 2 == 0, chip // 2, chips - 1 - chip // 2)
    return jnp.where(chip < half, chip, chips - 1 - (chip - half))


def kernel(
    n, nb, x_ref, flags_ref, band_ref, out_ref,
    w, rot, cos_ref, sin_ref, acc, energies, weight, part, got,
    ring_send, ring_recv, sib_send, sib_recv, en_send, en_recv, part_send, part_recv,
):
    rows, wide = x_ref.shape
    freq = wide // (2 * SEG)
    half = freq // 2
    depth = 2 * half
    chips = n // 2
    share = n * rows // nb
    me = lax.axis_index("sta")
    band = lax.axis_index("band")
    core = lax.rem(me, 2)
    pos = position_of(me // 2, chips)
    sibling = me + 1 - 2 * core

    def at_pos(offset, own_core):
        return station_of(lax.rem(pos + offset + chips, chips), own_core, chips)

    right, left = at_pos(1, core), at_pos(-1, core)

    barrier = pltpu.get_barrier_semaphore()
    for other in (right, left, sibling):
        pl.semaphore_signal(barrier, inc=1, device_id={"sta": other}, device_id_type=MESH)
    for k in range(1, nb):
        pl.semaphore_signal(
            barrier, inc=1, device_id={"band": lax.rem(band + k, nb)}, device_id_type=MESH
        )

    f_index = band * freq + lax.broadcasted_iota(jnp.int32, (rows, freq), 1)
    kept = (f_index >= band_ref[:, 0:1]) & (f_index < band_ref[:, 1:2])
    lane = lax.broadcasted_iota(jnp.int32, (rows, EXT), 1)
    sums, undo = [], []
    for g in range(SEG):
        vals = []
        for c in range(2):
            start = (g * 2 + c) * freq
            v = x_ref[:, start:start + freq].astype(jnp.float32)
            vals.append(jnp.where(kept, v, 0.0))
        e = jnp.sum(vals[0] * vals[0] + vals[1] * vals[1], axis=1, keepdims=True)
        big = jnp.where(e < 3.0e38, 2.0 ** -40, 0.0)
        fac = jnp.where(e < 2.0 ** -60, 2.0 ** 40, jnp.where(e > 2.0 ** 80, big, 1.0))
        undo.append(jnp.where(e < 2.0 ** -60, 2.0 ** -40, jnp.where(e > 2.0 ** 80, 2.0 ** 40, 1.0)))
        sums.append(e)
        for h in range(2):
            for c in range(2):
                w[2 * g + h, me, :, c * half:(c + 1) * half] = (
                    vals[c][:, h * half:(h + 1) * half] * fac
                ).astype(jnp.bfloat16)
    energies[band] = jnp.where(lane == 0, sums[0], jnp.where(lane == 1, sums[1], 0.0))

    pl.semaphore_wait(barrier, 3 + nb - 1)

    en_copies = []
    for k in range(1, nb):
        en_copies.append(pltpu.make_async_remote_copy(
            src_ref=energies.at[band], dst_ref=energies.at[band],
            send_sem=en_send.at[k], recv_sem=en_recv.at[k],
            device_id={"band": lax.rem(band + k, nb)}, device_id_type=MESH,
        ))
        en_copies[-1].start()

    def view(p, s):
        return w.at[p, s] if p == PIECES - 1 else w.at[p, s, :, 0:depth]

    def ring(p, way, t, s):
        return pltpu.make_async_remote_copy(
            src_ref=view(p, s), dst_ref=view(p, s),
            send_sem=ring_send.at[way, p, t], recv_sem=ring_recv.at[way, p, t],
            device_id={"sta": right if way == 0 else left}, device_id_type=MESH,
        )

    def across(p, k, s):
        return pltpu.make_async_remote_copy(
            src_ref=view(p, s), dst_ref=view(p, s),
            send_sem=sib_send.at[p, k], recv_sem=sib_recv.at[p, k],
            device_id={"sta": sibling}, device_id_type=MESH,
        )

    long = chips // 2
    hops = [(long, chips - 1 - long) if p % 2 == 0 else (chips - 1 - long, long)
            for p in range(PIECES)]
    sent = []

    def go(copy):
        copy.start()
        sent.append(copy)

    def send_own(p):
        for way in range(2):
            if hops[p][way] > 0:
                go(ring(p, way, 0, me))
        go(across(p, 0, me))

    send_own(0)
    send_own(1)
    send_own(2)

    for k in range(1, nb):
        source = lax.rem(band + nb - k, nb)
        pltpu.make_async_remote_copy(
            src_ref=energies.at[source], dst_ref=energies.at[source],
            send_sem=en_send.at[k], recv_sem=en_recv.at[k],
            device_id={"band": source}, device_id_type=MESH,
        ).wait_recv()
    total = energies[0]
    for k in range(1, nb):
        total = total + energies[k]
    width = (band_ref[:, 1:2] - band_ref[:, 0:1]).astype(jnp.float32)
    ext = jnp.zeros((rows, EXT), jnp.float32)
    own = []
    for g in range(SEG):
        valid = flags_ref[:, g:g + 1].astype(jnp.float32)
        factor = valid / jnp.sqrt(total[:, g:g + 1] / width + 1e-06) * undo[g]
        own.append(factor)
        rest = factor
        for i in range(3):
            term = rest.astype(jnp.bfloat16).astype(jnp.float32)
            rest = rest - term
            ext = jnp.where(lane == 3 * g + i, term, ext)
        ext = jnp.where(lane == 6 + g, valid, ext)
    w[PIECES - 1, me, :, depth:depth + EXT] = ext.astype(jnp.bfloat16)

    def phases(j):
        cols = pl.ds(pl.multiple_of(j * 128, 128), 128)
        lag = lax.broadcasted_iota(jnp.int32, (LAGS, 128), 0) - LAGS // 2
        f = band * freq + j * 128 + lax.broadcasted_iota(jnp.int32, (LAGS, 128), 1)
        turns = ((lag * f + FREQ // 2) & (FREQ - 1)) - FREQ // 2
        phase = turns.astype(jnp.float32) * (2.0 * math.pi / FREQ)
        cos_ref[:, cols] = jnp.cos(phase)
        sin_ref[:, cols] = jnp.sin(phase)

    def rotate(p, first, last):
        h = p % 2

        @pl.loop(first, last)
        def _(j):
            at = pl.multiple_of(j * 128, 128)
            table = pl.ds(pl.multiple_of(h * half + j * 128, 128), 128)
            cosine, sine = cos_ref[:, table], sin_ref[:, table]
            re = w[p, me, :, pl.ds(at, 128)].astype(jnp.float32)
            im = w[p, me, :, pl.ds(pl.multiple_of(half + j * 128, 128), 128)].astype(jnp.float32)
            for a in range(rows):
                r, i = re[a:a + 1], im[a:a + 1]
                lines = slice(a * LAGS, (a + 1) * LAGS)
                rot[p, lines, pl.ds(at, 128)] = (r * cosine - i * sine).astype(jnp.bfloat16)
                rot[p, lines, pl.ds(pl.multiple_of(half + j * 128, 128), 128)] = (
                    i * cosine + r * sine
                ).astype(jnp.bfloat16)

    def hop(p, t):
        for way in range(2):
            if t <= hops[p][way]:
                s = at_pos(-t if way == 0 else t, core)
                ring(p, way, t - 1, s).wait_recv()
                if t < hops[p][way]:
                    go(ring(p, way, t, s))
                go(across(p, t if way == 0 else hops[p][0] + t, s))

    def gathered(p):
        for k in range(chips):
            t = k if k <= hops[p][0] else k - hops[p][0]
            s = at_pos(-t if k <= hops[p][0] else t, 1 - core)
            across(p, k, s).wait_recv()

    def multiply(p, lines):
        g = p // 2
        step = min(depth, 512)

        @pl.loop(0, depth // step)
        def _(j):
            cols = pl.ds(pl.multiple_of(j * step, step), step)
            term = lax.dot_general(
                rot[p, lines, cols], w[p, :, :, cols].reshape(n * rows, step),
                (((1,), (1,)), ((), ())), preferred_element_type=jnp.float32,
            )
            if p % 2 == 0:
                @pl.when(j == 0)
                def _():
                    acc[g, lines] = term

                @pl.when(j > 0)
                def _():
                    acc[g, lines] += term
            else:
                acc[g, lines] += term

    order = sorted(
        ((p, t) for p in range(PIECES) for t in range(1, long + 1)),
        key=lambda pt: (pt[0] + pt[1], -pt[0]),
    )
    blocks = half // 128
    work = [functools.partial(pl.loop(blocks, 2 * blocks), phases)]
    for p in range(PIECES):
        work.append(functools.partial(rotate, p, 0, blocks // 2))
        work.append(functools.partial(rotate, p, blocks // 2, blocks))
    pl.loop(0, blocks)(phases)
    done = 0
    for index, (p, t) in enumerate(order):
        hop(p, t)
        if (p, t) == (0, 1):
            send_own(PIECES - 1)
        if work:
            work.pop(0)()
        if len(order) - index <= PIECES - 1:
            gathered(done)
            multiply(done, slice(0, rows * LAGS))
            done += 1
    gathered(PIECES - 1)

    ext_all = w[PIECES - 1, :, :, depth:depth + EXT].reshape(n * rows, EXT)
    row = lax.broadcasted_iota(jnp.int32, (16, EXT), 0)
    col = lax.broadcasted_iota(jnp.int32, (16, EXT), 1)
    pick = ((row < SEG) & (col >= 3 * row) & (col < 3 * row + 3)).astype(jnp.float32)
    nt = (((1,), (1,)), ((), ()))
    theirs = lax.dot_general(
        pick.astype(jnp.bfloat16), ext_all, nt, preferred_element_type=jnp.float32
    )
    flag_cols = jnp.where((lane >= 6) & (lane < 6 + SEG), ext, 0.0).astype(jnp.bfloat16)
    pairs = lax.dot_general(flag_cols, ext_all, nt, preferred_element_type=jnp.float32)
    denominator = 1.0 / (jnp.maximum(pairs, 1.0) * math.sqrt(FREQ))
    for g in range(SEG):
        weight[g] = own[g] * theirs[g:g + 1] * denominator

    def stack(q, first, last):
        cols = pl.ds(pl.multiple_of(q * share, share), share)
        left_factor, right_factor = weight[0, :, cols], weight[1, :, cols]
        for a in range(first, last):
            lines = slice(a * LAGS, (a + 1) * LAGS)
            part[q, lines] = (
                acc[0, lines, cols] * left_factor[a:a + 1]
                + acc[1, lines, cols] * right_factor[a:a + 1]
            )

    copies = []
    for m in range(2):
        first, last = m * rows // 2, (m + 1) * rows // 2
        lines = slice(first * LAGS, last * LAGS)
        multiply(PIECES - 1, lines)
        for k in range(1, nb):
            target = lax.rem(band + k, nb)
            stack(target, first, last)
            copies.append(pltpu.make_async_remote_copy(
                src_ref=part.at[target, lines], dst_ref=got.at[k, lines],
                send_sem=part_send.at[k, m], recv_sem=part_recv.at[k, m],
                device_id={"band": target}, device_id_type=MESH,
            ))
            copies[-1].start()
    stack(band, 0, rows)
    for copy in sent + en_copies:
        copy.wait_send()
    for m in range(2):
        lines = slice(m * rows // 2 * LAGS, (m + 1) * rows // 2 * LAGS)
        for copy in copies[m * (nb - 1):(m + 1) * (nb - 1)]:
            copy.wait()
        result = part[band, lines]
        for k in range(1, nb):
            result = result + got[k, lines]
        out_ref[lines] = result


def solution(mesh):
    n, nb = mesh.shape["sta"], mesh.shape["band"]

    def local(spectra, flags, passband):
        rows, _, _, freq = spectra.shape
        share = n * rows // nb
        depth = freq
        vmem = pl.BlockSpec(memory_space=pltpu.VMEM)
        chips = n // 2
        dma = pltpu.SemaphoreType.DMA
        out = pl.pallas_call(
            functools.partial(kernel, n, nb),
            out_shape=jax.ShapeDtypeStruct((rows * LAGS, share), jnp.float32),
            in_specs=[vmem] * 3,
            out_specs=vmem,
            scratch_shapes=[
                pltpu.VMEM((PIECES, n, rows, depth + EXT), jnp.bfloat16),
                pltpu.VMEM((PIECES, rows * LAGS, depth), jnp.bfloat16),
                pltpu.VMEM((LAGS, freq), jnp.float32),
                pltpu.VMEM((LAGS, freq), jnp.float32),
                pltpu.VMEM((SEG, rows * LAGS, n * rows), jnp.float32),
                pltpu.VMEM((nb, rows, EXT), jnp.float32),
                pltpu.VMEM((SEG, rows, n * rows), jnp.float32),
                pltpu.VMEM((nb, rows * LAGS, share), jnp.float32),
                pltpu.VMEM((nb, rows * LAGS, share), jnp.float32),
                dma((2, PIECES, chips)), dma((2, PIECES, chips)),
                dma((PIECES, chips)), dma((PIECES, chips)),
                dma((nb,)), dma((nb,)), dma((nb, 2)), dma((nb, 2)),
            ],
            compiler_params=pltpu.CompilerParams(
                collective_id=0, has_side_effects=True, vmem_limit_bytes=48 * 1024 * 1024
            ),
        )(spectra.reshape(rows, SEG * 2 * freq), flags, passband)
        return out.reshape(rows, LAGS, share)

    placed = (P("sta", None, None, "band"), P("sta", None), P("sta", None))
    return jax.shard_map(
        local, mesh=mesh, in_specs=placed, out_specs=P("sta", None, "band"), check_vma=False
    )
```

```python
import functools
import math

import jax
import jax.numpy as jnp
from jax import lax
from jax.experimental import pallas as pl
from jax.experimental.pallas import tpu as pltpu
from jax.sharding import PartitionSpec as P

FREQ = 4096
LAGS = 32
SEG = 2
PIECES = 4
EXT = 128
MESH = pl.DeviceIdType.MESH


def station_of(position, core, chips):
    half = chips // 2
    if chips == 8:
        chip = jnp.where(position < half, 2 * position, 2 * (chips - 1 - position) + 1)
    else:
        chip = jnp.where(position < half, position, half + (chips - 1 - position))
    return 2 * chip + core


def position_of(chip, chips):
    half = chips // 2
    if chips == 8:
        return jnp.where(chip % 2 == 0, chip // 2, chips - 1 - chip // 2)
    return jnp.where(chip < half, chip, chips - 1 - (chip - half))


def kernel(
    n, nb, x_ref, flags_ref, band_ref, out_ref,
    w, rot, cos_ref, sin_ref, acc, energies, weight, part, got,
    ring_send, ring_recv, sib_send, sib_recv, en_send, en_recv, part_send, part_recv,
):
    rows, wide = x_ref.shape
    freq = wide // (2 * SEG)
    half = freq // 2
    depth = 2 * half
    chips = n // 2
    share = n * rows // nb
    me = lax.axis_index("sta")
    band = lax.axis_index("band")
    core = lax.rem(me, 2)
    pos = position_of(me // 2, chips)
    sibling = me + 1 - 2 * core

    def at_pos(offset, own_core):
        return station_of(lax.rem(pos + offset + chips, chips), own_core, chips)

    right, left = at_pos(1, core), at_pos(-1, core)

    barrier = pltpu.get_barrier_semaphore()
    for other in (right, left, sibling):
        pl.semaphore_signal(barrier, inc=1, device_id={"sta": other}, device_id_type=MESH)
    for k in range(1, nb):
        pl.semaphore_signal(
            barrier, inc=1, device_id={"band": lax.rem(band + k, nb)}, device_id_type=MESH
        )

    f_index = band * freq + lax.broadcasted_iota(jnp.int32, (rows, freq), 1)
    kept = (f_index >= band_ref[:, 0:1]) & (f_index < band_ref[:, 1:2])
    lane = lax.broadcasted_iota(jnp.int32, (rows, EXT), 1)
    sums, undo = [], []
    for g in range(SEG):
        vals = []
        for c in range(2):
            start = (g * 2 + c) * freq
            v = x_ref[:, start:start + freq].astype(jnp.float32)
            vals.append(jnp.where(kept, v, 0.0))
        e = jnp.sum(vals[0] * vals[0] + vals[1] * vals[1], axis=1, keepdims=True)
        big = jnp.where(e < 3.0e38, 2.0 ** -40, 0.0)
        fac = jnp.where(e < 2.0 ** -60, 2.0 ** 40, jnp.where(e > 2.0 ** 80, big, 1.0))
        undo.append(jnp.where(e < 2.0 ** -60, 2.0 ** -40, jnp.where(e > 2.0 ** 80, 2.0 ** 40, 1.0)))
        sums.append(e)
        for h in range(2):
            for c in range(2):
                w[2 * g + h, me, :, c * half:(c + 1) * half] = (
                    vals[c][:, h * half:(h + 1) * half] * fac
                ).astype(jnp.bfloat16)
    energies[band] = jnp.where(lane == 0, sums[0], jnp.where(lane == 1, sums[1], 0.0))

    pl.semaphore_wait(barrier, 3 + nb - 1)

    en_copies = []
    for k in range(1, nb):
        en_copies.append(pltpu.make_async_remote_copy(
            src_ref=energies.at[band], dst_ref=energies.at[band],
            send_sem=en_send.at[k], recv_sem=en_recv.at[k],
            device_id={"band": lax.rem(band + k, nb)}, device_id_type=MESH,
        ))
        en_copies[-1].start()

    def view(p, s):
        return w.at[p, s] if p == PIECES - 1 else w.at[p, s, :, 0:depth]

    def ring(p, way, t, s):
        return pltpu.make_async_remote_copy(
            src_ref=view(p, s), dst_ref=view(p, s),
            send_sem=ring_send.at[way, p, t], recv_sem=ring_recv.at[way, p, t],
            device_id={"sta": right if way == 0 else left}, device_id_type=MESH,
        )

    def across(p, k, s):
        return pltpu.make_async_remote_copy(
            src_ref=view(p, s), dst_ref=view(p, s),
            send_sem=sib_send.at[p, k], recv_sem=sib_recv.at[p, k],
            device_id={"sta": sibling}, device_id_type=MESH,
        )

    long = chips // 2
    hops = [(long, chips - 1 - long) if p % 2 == 0 else (chips - 1 - long, long)
            for p in range(PIECES)]
    sent = []

    def go(copy):
        copy.start()
        sent.append(copy)

    def send_own(p):
        for way in range(2):
            if hops[p][way] > 0:
                go(ring(p, way, 0, me))
        go(across(p, 0, me))

    send_own(0)
    send_own(1)
    send_own(2)

    for k in range(1, nb):
        source = lax.rem(band + nb - k, nb)
        pltpu.make_async_remote_copy(
            src_ref=energies.at[source], dst_ref=energies.at[source],
            send_sem=en_send.at[k], recv_sem=en_recv.at[k],
            device_id={"band": source}, device_id_type=MESH,
        ).wait_recv()
    total = energies[0]
    for k in range(1, nb):
        total = total + energies[k]
    width = (band_ref[:, 1:2] - band_ref[:, 0:1]).astype(jnp.float32)
    ext = jnp.zeros((rows, EXT), jnp.float32)
    own = []
    for g in range(SEG):
        valid = flags_ref[:, g:g + 1].astype(jnp.float32)
        factor = valid / jnp.sqrt(total[:, g:g + 1] / width + 1e-06) * undo[g]
        own.append(factor)
        rest = factor
        for i in range(3):
            term = rest.astype(jnp.bfloat16).astype(jnp.float32)
            rest = rest - term
            ext = jnp.where(lane == 3 * g + i, term, ext)
        ext = jnp.where(lane == 6 + g, valid, ext)
    w[PIECES - 1, me, :, depth:depth + EXT] = ext.astype(jnp.bfloat16)

    def phases(j):
        cols = pl.ds(pl.multiple_of(j * 128, 128), 128)
        lag = lax.broadcasted_iota(jnp.int32, (LAGS, 128), 0) - LAGS // 2
        f = band * freq + j * 128 + lax.broadcasted_iota(jnp.int32, (LAGS, 128), 1)
        turns = ((lag * f + FREQ // 2) & (FREQ - 1)) - FREQ // 2
        phase = turns.astype(jnp.float32) * (2.0 * math.pi / FREQ)
        cos_ref[:, cols] = jnp.cos(phase)
        sin_ref[:, cols] = jnp.sin(phase)

    def rotate(p, first, last):
        h = p % 2

        @pl.loop(first, last)
        def _(j):
            at = pl.multiple_of(j * 128, 128)
            table = pl.ds(pl.multiple_of(h * half + j * 128, 128), 128)
            cosine, sine = cos_ref[:, table], sin_ref[:, table]
            re = w[p, me, :, pl.ds(at, 128)].astype(jnp.float32)
            im = w[p, me, :, pl.ds(pl.multiple_of(half + j * 128, 128), 128)].astype(jnp.float32)
            for a in range(rows):
                r, i = re[a:a + 1], im[a:a + 1]
                lines = slice(a * LAGS, (a + 1) * LAGS)
                rot[p, lines, pl.ds(at, 128)] = (r * cosine - i * sine).astype(jnp.bfloat16)
                rot[p, lines, pl.ds(pl.multiple_of(half + j * 128, 128), 128)] = (
                    i * cosine + r * sine
                ).astype(jnp.bfloat16)

    def hop(p, t):
        for way in range(2):
            if t <= hops[p][way]:
                s = at_pos(-t if way == 0 else t, core)
                ring(p, way, t - 1, s).wait_recv()
                if t < hops[p][way]:
                    go(ring(p, way, t, s))
                go(across(p, t if way == 0 else hops[p][0] + t, s))

    def gathered(p):
        for k in range(chips):
            t = k if k <= hops[p][0] else k - hops[p][0]
            s = at_pos(-t if k <= hops[p][0] else t, 1 - core)
            across(p, k, s).wait_recv()

    def multiply(p, lines):
        g = p // 2
        step = min(depth, 512)

        @pl.loop(0, depth // step)
        def _(j):
            cols = pl.ds(pl.multiple_of(j * step, step), step)
            term = lax.dot_general(
                rot[p, lines, cols], w[p, :, :, cols].reshape(n * rows, step),
                (((1,), (1,)), ((), ())), preferred_element_type=jnp.float32,
            )
            if p % 2 == 0:
                @pl.when(j == 0)
                def _():
                    acc[g, lines] = term

                @pl.when(j > 0)
                def _():
                    acc[g, lines] += term
            else:
                acc[g, lines] += term

    waiting, order = [(p, 1) for p in range(PIECES - 1)], []
    while waiting:
        p, t = waiting.pop(0)
        order.append((p, t))
        if t < long:
            waiting.append((p, t + 1))
        if (p, t) == (0, 1):
            waiting.append((PIECES - 1, 1))
    blocks = half // 128
    work = [functools.partial(pl.loop(blocks, 2 * blocks), phases)]
    for p in range(PIECES):
        work.append(functools.partial(rotate, p, 0, blocks // 2))
        work.append(functools.partial(rotate, p, blocks // 2, blocks))
    pl.loop(0, blocks)(phases)
    done = 0
    for index, (p, t) in enumerate(order):
        hop(p, t)
        if (p, t) == (0, 1):
            send_own(PIECES - 1)
        if work:
            work.pop(0)()
        if len(order) - index <= PIECES - 1:
            gathered(done)
            multiply(done, slice(0, rows * LAGS))
            done += 1
    gathered(PIECES - 1)

    ext_all = w[PIECES - 1, :, :, depth:depth + EXT].reshape(n * rows, EXT)
    row = lax.broadcasted_iota(jnp.int32, (16, EXT), 0)
    col = lax.broadcasted_iota(jnp.int32, (16, EXT), 1)
    pick = ((row < SEG) & (col >= 3 * row) & (col < 3 * row + 3)).astype(jnp.float32)
    nt = (((1,), (1,)), ((), ()))
    theirs = lax.dot_general(
        pick.astype(jnp.bfloat16), ext_all, nt, preferred_element_type=jnp.float32
    )
    flag_cols = jnp.where((lane >= 6) & (lane < 6 + SEG), ext, 0.0).astype(jnp.bfloat16)
    pairs = lax.dot_general(flag_cols, ext_all, nt, preferred_element_type=jnp.float32)
    denominator = 1.0 / (jnp.maximum(pairs, 1.0) * math.sqrt(FREQ))
    for g in range(SEG):
        weight[g] = own[g] * theirs[g:g + 1] * denominator

    def stack(q, first, last):
        cols = pl.ds(pl.multiple_of(q * share, share), share)
        left_factor, right_factor = weight[0, :, cols], weight[1, :, cols]
        for a in range(first, last):
            lines = slice(a * LAGS, (a + 1) * LAGS)
            part[q, lines] = (
                acc[0, lines, cols] * left_factor[a:a + 1]
                + acc[1, lines, cols] * right_factor[a:a + 1]
            )

    copies = []
    for m in range(2):
        first, last = m * rows // 2, (m + 1) * rows // 2
        lines = slice(first * LAGS, last * LAGS)
        multiply(PIECES - 1, lines)
        for k in range(1, nb):
            target = lax.rem(band + k, nb)
            stack(target, first, last)
            copies.append(pltpu.make_async_remote_copy(
                src_ref=part.at[target, lines], dst_ref=got.at[k, lines],
                send_sem=part_send.at[k, m], recv_sem=part_recv.at[k, m],
                device_id={"band": target}, device_id_type=MESH,
            ))
            copies[-1].start()
    stack(band, 0, rows)
    for copy in sent + en_copies:
        copy.wait_send()
    for m in range(2):
        lines = slice(m * rows // 2 * LAGS, (m + 1) * rows // 2 * LAGS)
        for copy in copies[m * (nb - 1):(m + 1) * (nb - 1)]:
            copy.wait()
        result = part[band, lines]
        for k in range(1, nb):
            result = result + got[k, lines]
        out_ref[lines] = result


def solution(mesh):
    n, nb = mesh.shape["sta"], mesh.shape["band"]

    def local(spectra, flags, passband):
        rows, _, _, freq = spectra.shape
        share = n * rows // nb
        depth = freq
        vmem = pl.BlockSpec(memory_space=pltpu.VMEM)
        chips = n // 2
        dma = pltpu.SemaphoreType.DMA
        out = pl.pallas_call(
            functools.partial(kernel, n, nb),
            out_shape=jax.ShapeDtypeStruct((rows * LAGS, share), jnp.float32),
            in_specs=[vmem] * 3,
            out_specs=vmem,
            scratch_shapes=[
                pltpu.VMEM((PIECES, n, rows, depth + EXT), jnp.bfloat16),
                pltpu.VMEM((PIECES, rows * LAGS, depth), jnp.bfloat16),
                pltpu.VMEM((LAGS, freq), jnp.float32),
                pltpu.VMEM((LAGS, freq), jnp.float32),
                pltpu.VMEM((SEG, rows * LAGS, n * rows), jnp.float32),
                pltpu.VMEM((nb, rows, EXT), jnp.float32),
                pltpu.VMEM((SEG, rows, n * rows), jnp.float32),
                pltpu.VMEM((nb, rows * LAGS, share), jnp.float32),
                pltpu.VMEM((nb, rows * LAGS, share), jnp.float32),
                dma((2, PIECES, chips)), dma((2, PIECES, chips)),
                dma((PIECES, chips)), dma((PIECES, chips)),
                dma((nb,)), dma((nb,)), dma((nb, 2)), dma((nb, 2)),
            ],
            compiler_params=pltpu.CompilerParams(
                collective_id=0, has_side_effects=True, vmem_limit_bytes=48 * 1024 * 1024
            ),
        )(spectra.reshape(rows, SEG * 2 * freq), flags, passband)
        return out.reshape(rows, LAGS, share)

    placed = (P("sta", None, None, "band"), P("sta", None), P("sta", None))
    return jax.shard_map(
        local, mesh=mesh, in_specs=placed, out_specs=P("sta", None, "band"), check_vma=False
    )
```
